32 devices in a mesh: section: 4 (over y, x), expert: 8 (over z, core).
Axes of the slice: x: 2, y: 2, z: 4, core: 2. Of those that a mesh axis runs over, the one named last changes fastest.
Arguments:
- fwd_arriving: bfloat16 [4, 256, 7168], P('section', 'expert'), may hold values from -6 to 6
- fwd_entering: bfloat16 [1, 256, 7168], P(None, 'expert'), may hold values from -6 to 6
- bwd_arriving: bfloat16 [4, 256, 7168], P('section', 'expert'), may hold values from -6 to 6
- bwd_entering: bfloat16 [1, 256, 7168], P(None, 'expert'), may hold values from -6 to 6
- saved_inputs: bfloat16 [4, 2, 256, 7168], P('section', None, 'expert'), may hold values from -6 to 6
- w_gate: bfloat16 [4, 8, 7168, 512], P('section', 'expert'), may hold values from -0.0625 to 0.0625
- w_up: bfloat16 [4, 8, 7168, 512], P('section', 'expert'), may hold values from -0.0625 to 0.0625
- w_down: bfloat16 [4, 8, 512, 7168], P('section', 'expert'), may hold values from -0.1875 to 0.1875
- route_ids: int32 [2, 4, 2, 256, 2], P(None, 'section', None, 'expert'), may hold values from 0 to 3, all different within a row; in each aligned block of 32 rows (0 to 31, 32 to 63, ..., all dimensions but the last counted through in order) at most 24 rows name the same one
- gate_levels: int32 [2, 4, 2, 256, 2], P(None, 'section', None, 'expert'), may hold values from 1 to 16
- token_counts: int32 [2, 5, 8], P(None, None, 'expert'), may hold values from 1 to 32, 224 in all within a row
Outputs:
- fwd_outputs: bfloat16 [4, 2, 256, 7168], P('section', None, 'expert')
- bwd_outputs: bfloat16 [4, 2, 256, 7168], P('section', None, 'expert')
The draws below stay inside these ranges and needn't reach their ends.
Inputs may be any that keep to these rules, and one draw needn't show every extreme that they name: `route_ids`: each token names 2 different experts; among the 32 tokens of one device for one direction, section and step no expert is named by more than 24 tokens. `token_counts`: the first so many token slots of a device are live; for each direction and micro-batch the counts over the devices sum to 224 and the largest is 32.
All inputs are finite; a program needn't handle non-finite values.
Results may differ from the reference program's by a relative error of at most 0.009.
Values may be sent and summed in bfloat16 or wider, within the bound.
No kernel may reach another device: no remote copies, remote signals or barrier semaphores. Data moves between devices by JAX's collectives and lax.ppermute only.
A program may use at most 192 MiB of HBM per device.

```python
import math
from functools import partial
import jax
import jax.numpy as jnp
import numpy as np
from jax import lax

D = 7168
HID = 1024
SLICES = 2
TOPK = 2
TICKS = 2
TOK_DEV = 32
SECTIONS = 4
PIECES = 8
EXPERTS = 4
H_DEV = 512
CAP = 24
TOKENS = 256
MBS = 5
N_EXPERT = 8


def place_ends(entries, own_key, low, top_value):
    place = [jax.random.randint(jax.random.fold_in(own_key, axis), (), 0, length) for axis, length in enumerate(entries.shape)]
    main_axis = entries.shape.index(max(entries.shape))
    next_to = place[:main_axis] + [(place[main_axis] + 1) % entries.shape[main_axis]] + place[main_axis + 1:]
    return entries.at[tuple(place)].set(low).at[tuple(next_to)].set(top_value)


def level_of(own_key, shape, split, least, high):
    loudness, own = 1.0, jax.random.fold_in(own_key, 6)
    for axis_at, blocks in split:
        heights = jnp.exp(jax.random.uniform(jax.random.fold_in(own, axis_at), (blocks,), jnp.float32, least / len(split), high / len(split)))
        loudness = loudness * jnp.repeat(heights, shape[axis_at] // blocks).reshape([-1 if axis == axis_at else 1 for axis in range(len(shape))])
    return loudness


def length_profile(amount, total, most, skew):
    loads = [(1 << 20) // math.isqrt(rank ** skew) + 1 for rank in range(2, amount + 1)]
    surplus, given = total - most - (amount - 1), [1] * (amount - 1)
    while surplus > 0:
        free = [i for i in range(amount - 1) if given[i] < most]
        mass, budget = sum([loads[i] for i in free]), surplus
        for i in free:
            addition = min(most - given[i], max(1, budget * loads[i] // mass), surplus)
            given[i] = given[i] + addition
            surplus = surplus - addition
    return np.array([most] + given)


def ragged(own_key, count, total, most, skew):
    if count == 2:
        one = jax.random.randint(own_key, (), max(1, total - most), min(most, total - 1) + 1)
        return jnp.stack([one, total - one])
    lengths = jnp.asarray(length_profile(count, total, most, skew), jnp.int32)
    pairs = (count - 1) // 2
    donor, receiver = lengths[1:1 + 2 * pairs:2], lengths[2:2 + 2 * pairs:2]
    margin = jnp.minimum(donor - 1, most - receiver)
    passed = jax.random.randint(jax.random.fold_in(own_key, 1), (pairs,), 0, 1 << 20) % (margin + 1)
    lengths = lengths.at[1:1 + 2 * pairs:2].set(donor - passed).at[2:2 + 2 * pairs:2].set(receiver + passed)
    return lengths[jax.random.permutation(jax.random.fold_in(own_key, 2), count)]


def deal_out(own_key, own, number, rows, count, top, limit, skew):
    sequence = jax.random.permutation(own_key, count)
    heavy_load, ordinary = portions_of(count, rows * top, limit, skew, True), portions_of(count, rows * top, limit, skew, False)
    places = jnp.arange(count)

    def named(tallies, rotation):
        used = int((tallies > 0).sum())
        fixed = max(1, used // 4)
        shifted = fixed + (places - fixed + rotation * (used - fixed)) % max(1, count - fixed)
        return jnp.zeros((count,), jnp.int32).at[sequence[jnp.where(places < fixed, places, shifted)]].set(jnp.asarray(tallies, jnp.int32))

    tallies = jnp.where(number % 4 == 0, named(heavy_load, number // 4), named(ordinary, number - number // 4 - 1))
    mixed = jax.random.permutation(jax.random.fold_in(own, 3), count)
    donor, receiver = mixed[0:count // 2 * 2:2], mixed[1:count // 2 * 2:2]
    margin = jnp.minimum(tallies[donor] - 1, limit - tallies[receiver]) // 2
    margin = jnp.where((donor == sequence[0]) | (receiver == sequence[0]) | (tallies[receiver] == 0), 0, jnp.maximum(margin, 0))
    shifted = jax.random.randint(jax.random.fold_in(own, 4), (count // 2,), 0, 1 << 20) % (margin + 1)
    tallies = tallies.at[donor].add(-shifted).at[receiver].add(shifted)
    labels = jnp.searchsorted(jnp.cumsum(tallies), jnp.arange(rows * top), side="right").astype(jnp.int32)
    listing = labels.reshape(top, rows).T
    listing = listing[jax.random.permutation(jax.random.fold_in(own, 1), rows)]
    rotation = jax.random.randint(jax.random.fold_in(own, 2), (rows, 1), 0, top)
    return jnp.take_along_axis(listing, (jnp.arange(top)[None, :] + rotation) % top, axis=1)


def portions_of(amount, total, bound, lean, full):
    loads = [(1 << 20) // math.isqrt(standing ** lean) + 1 for standing in range(1, amount + 1)]
    largest = bound if full else min(bound, max(-(-total // amount), total * loads[0] // sum(loads)))
    least = 1 if total - largest >= amount - 1 else 0
    counts, surplus = [largest] + [least] * (amount - 1), total - largest - least * (amount - 1)
    while surplus > 0:
        free = [i for i in range(1, amount) if counts[i] < largest] or [i for i in range(1, amount) if counts[i] < bound]
        mass, left = sum([loads[i] for i in free]), surplus
        for i in free:
            extra = min(bound - counts[i], max(1, left * loads[i] // mass), surplus)
            counts[i] = counts[i] + extra
            surplus = surplus - extra
    return np.array(counts)


def bell_draw(rng, dims, deviation, bound, split=(), held_as=jnp.bfloat16):
    level = level_of(rng, dims, split, -0.22, 0.18) if split else 1.0
    drawn = jax.random.normal(rng, dims, jnp.float32) * deviation * level
    return jnp.minimum(jnp.maximum(drawn, -bound), bound).astype(held_as)


def setup_inputs(seed: int = 0) -> dict:
    key_of = jax.random.split(jax.random.key(seed), 12)
    fwd_arriving = bell_draw(key_of[0], (SECTIONS, TOKENS, D), 1.0, 6.0, ((0, 4), (1, 8)))
    fwd_entering = bell_draw(key_of[1], (TICKS - 1, TOKENS, D), 1.0, 6.0, ((1, 8),))
    bwd_arriving = bell_draw(key_of[2], (SECTIONS, TOKENS, D), 1.0, 6.0, ((0, 4), (1, 8)))
    bwd_entering = bell_draw(key_of[3], (TICKS - 1, TOKENS, D), 1.0, 6.0, ((1, 8),))
    saved_inputs = bell_draw(key_of[4], (SECTIONS, TICKS, TOKENS, D), 1.0, 6.0, ((0, 4), (2, 8)))
    w_gate = bell_draw(key_of[5], (SECTIONS, PIECES, D, H_DEV), D ** -0.5, 0.0625, ((0, 4), (1, 8)))
    w_up = bell_draw(key_of[6], (SECTIONS, PIECES, D, H_DEV), D ** -0.5, 0.0625, ((0, 4), (1, 8)))
    w_down = bell_draw(key_of[7], (SECTIONS, PIECES, H_DEV, D), HID ** -0.5, 0.1875, ((0, 4), (1, 8)))
    route_ids_keys = jax.random.split(jax.random.fold_in(key_of[8], 1), 2 * SECTIONS * TICKS * TOKENS // TOK_DEV)
    route_ids_turns = jax.random.permutation(jax.random.fold_in(key_of[8], 3), 2 * SECTIONS * TICKS * TOKENS // TOK_DEV)
    route_ids = jax.vmap(lambda own, number: deal_out(jax.random.fold_in(key_of[8], 2), own, number, TOK_DEV, EXPERTS, TOPK, CAP, 2))(route_ids_keys, route_ids_turns).reshape((2, SECTIONS, TICKS, TOKENS, TOPK))
    gate_levels = place_ends(jax.random.randint(key_of[9], (2, SECTIONS, TICKS, TOKENS, TOPK), 1, 17), jax.random.fold_in(key_of[9], 1), 1, 16).astype(jnp.int32)
    token_counts = jax.vmap(lambda own: ragged(own, PIECES, TOK_DEV * N_EXPERT * 7 // 8, TOK_DEV, 2))(jax.random.split(key_of[10], 2 * MBS)).reshape((2, MBS, PIECES)).astype(jnp.int32)
    return {"fwd_arriving": fwd_arriving, "fwd_entering": fwd_entering, "bwd_arriving": bwd_arriving, "bwd_entering": bwd_entering, "saved_inputs": saved_inputs, "w_gate": w_gate, "w_up": w_up, "w_down": w_down, "route_ids": route_ids, "gate_levels": gate_levels, "token_counts": token_counts}


def route_slots(route_row, level_row, live_count, experts_win, capacity):
    token_total = route_row.shape[0]
    topk_count = route_row.shape[1]
    live_mask = (jnp.arange(token_total, dtype=jnp.int32) < live_count).astype(jnp.int32)
    onehot = (route_row[:, :, None] == jnp.arange(experts_win, dtype=jnp.int32)[None, None, :]).astype(jnp.int32)
    onehot = onehot * live_mask[:, None, None]
    onehot_flat = onehot.reshape(token_total * topk_count, experts_win)
    before = jnp.cumsum(onehot_flat, axis=0) - onehot_flat
    position = jnp.sum(before * onehot_flat, axis=1).reshape(token_total, topk_count)
    target = jnp.where(live_mask[:, None] > 0, route_row * capacity + position, experts_win * capacity).astype(jnp.int32)
    level_float = level_row.astype(jnp.float32)
    gate_weight = level_float / jnp.sum(level_float, axis=1, keepdims=True)
    return target, gate_weight * live_mask[:, None].astype(jnp.float32)


def pack_rows(row_block, target, experts_win, capacity):
    token_total, topk_count = target.shape
    features = row_block.shape[1]
    holder = jnp.zeros((experts_win * capacity + 1, features), row_block.dtype)
    copies = jnp.broadcast_to(row_block[:, None, :], (token_total, topk_count, features)).reshape(token_total * topk_count, features)
    holder = holder.at[target.reshape(-1)].set(copies)
    return holder[: experts_win * capacity]


def unpack_rows(returned, target, gate_weight):
    holder = jnp.concatenate([returned, jnp.zeros((1, returned.shape[1]), returned.dtype)], axis=0)
    picked = holder[target]
    return jnp.sum(picked * gate_weight[:, :, None], axis=1)


def piece_forward(row_block, gate_piece, up_piece, down_piece):
    gate_pre = jnp.dot(row_block, gate_piece, preferred_element_type=jnp.float32)
    up_pre = jnp.dot(row_block, up_piece, preferred_element_type=jnp.float32)
    hidden = (jax.nn.silu(gate_pre) * up_pre).astype(jnp.bfloat16)
    return jnp.dot(hidden, down_piece, preferred_element_type=jnp.float32).astype(jnp.bfloat16)


def piece_backward(row_block, grad_block, gate_piece, up_piece, down_piece):
    gate_pre = jnp.dot(row_block, gate_piece, preferred_element_type=jnp.float32)
    up_pre = jnp.dot(row_block, up_piece, preferred_element_type=jnp.float32)
    d_hidden = jnp.dot(grad_block, down_piece.T, preferred_element_type=jnp.float32)
    sigmoid_gate = jax.nn.sigmoid(gate_pre)
    d_up = (d_hidden * gate_pre * sigmoid_gate).astype(jnp.bfloat16)
    d_gate = (d_hidden * up_pre * sigmoid_gate * (1.0 + gate_pre * (1.0 - sigmoid_gate))).astype(jnp.bfloat16)
    back_share = jnp.dot(d_gate, gate_piece.T, preferred_element_type=jnp.float32)
    back_share = back_share + jnp.dot(d_up, up_piece.T, preferred_element_type=jnp.float32)
    return back_share.astype(jnp.bfloat16)


def expert_layer(section_index, row_inputs, row_grads, route_slab, level_slab, count_row, w_gate, w_up, w_down):
    sources = count_row.shape[0]
    slotter = partial(route_slots, experts_win=EXPERTS, capacity=CAP)
    targets, gates = jax.vmap(slotter)(route_slab.reshape(sources, TOK_DEV, TOPK), level_slab.reshape(sources, TOK_DEV, TOPK), count_row)
    packer = jax.vmap(partial(pack_rows, experts_win=EXPERTS, capacity=CAP))

    def regroup(row_array):
        packed = packer(row_array.reshape(sources, TOK_DEV, D), targets)
        return packed.reshape(sources, EXPERTS, CAP, D).transpose(1, 0, 2, 3).reshape(EXPERTS, sources * CAP, D)

    inputs_by_expert = regroup(row_inputs)
    grads_by_expert = inputs_by_expert if row_grads is None else regroup(row_grads)
    gate_section = w_gate[section_index]
    up_section = w_up[section_index]
    down_section = w_down[section_index]

    def one_expert(expert_index):
        rows_here = lax.dynamic_index_in_dim(inputs_by_expert, expert_index, 0, keepdims=False)
        grads_here = lax.dynamic_index_in_dim(grads_by_expert, expert_index, 0, keepdims=False)
        running = jnp.zeros((sources * CAP, D), jnp.float32)
        for piece_index in range(SLICES):
            slot_index = (expert_index * SLICES + piece_index).astype(jnp.int32)
            gate_piece = lax.dynamic_index_in_dim(gate_section, slot_index, 0, keepdims=False)
            up_piece = lax.dynamic_index_in_dim(up_section, slot_index, 0, keepdims=False)
            down_piece = lax.dynamic_index_in_dim(down_section, slot_index, 0, keepdims=False)
            if row_grads is None:
                piece_share = piece_forward(rows_here, gate_piece, up_piece, down_piece)
            else:
                piece_share = piece_backward(rows_here, grads_here, gate_piece, up_piece, down_piece)
            running = running + piece_share.astype(jnp.float32)
        return running

    shares = lax.map(one_expert, jnp.arange(EXPERTS, dtype=jnp.int32))
    shares = shares.reshape(EXPERTS, sources, CAP, D).transpose(1, 0, 2, 3).reshape(sources, EXPERTS * CAP, D)
    combined = jax.vmap(unpack_rows)(shares, targets, gates).reshape(sources * TOK_DEV, D)
    residual = row_inputs if row_grads is None else row_grads
    return (residual.astype(jnp.float32) + combined).astype(jnp.bfloat16)


def reference(fwd_arriving, fwd_entering, bwd_arriving, bwd_entering, saved_inputs, w_gate, w_up, w_down, route_ids, gate_levels, token_counts):
    fwd_results = {}
    bwd_results = {}
    for tick_index in range(TICKS):
        for section_index in range(SECTIONS):
            if tick_index == 0:
                layer_in = fwd_arriving[section_index]
            elif section_index == 0:
                layer_in = fwd_entering[tick_index - 1]
            else:
                layer_in = fwd_results[(section_index - 1, tick_index - 1)]
            batch_index = tick_index - section_index + SECTIONS - 1
            fwd_results[(section_index, tick_index)] = expert_layer(section_index, layer_in, None, route_ids[0, section_index, tick_index], gate_levels[0, section_index, tick_index], token_counts[0, batch_index], w_gate, w_up, w_down)
        for section_index in range(SECTIONS - 1, -1, -1):
            if tick_index == 0:
                grad_in = bwd_arriving[section_index]
            elif section_index == SECTIONS - 1:
                grad_in = bwd_entering[tick_index - 1]
            else:
                grad_in = bwd_results[(section_index + 1, tick_index - 1)]
            batch_index = tick_index + section_index
            bwd_results[(section_index, tick_index)] = expert_layer(section_index, saved_inputs[section_index, tick_index], grad_in, route_ids[1, section_index, tick_index], gate_levels[1, section_index, tick_index], token_counts[1, batch_index], w_gate, w_up, w_down)
    fwd_outputs = jnp.stack([jnp.stack([fwd_results[(section_index, tick_index)] for tick_index in range(TICKS)]) for section_index in range(SECTIONS)])
    bwd_outputs = jnp.stack([jnp.stack([bwd_results[(section_index, tick_index)] for tick_index in range(TICKS)]) for section_index in range(SECTIONS)])
    return fwd_outputs, bwd_outputs
```

```python
import jax
import jax.numpy as jnp
from jax import lax
from jax.experimental import pallas as pl
from jax.experimental.pallas import tpu as pltpu
from jax.sharding import PartitionSpec as P

SLICES = 2
TICKS = 2
LINE = 4
TILE = 1024
VMEM_LIMIT = 48 * 1024 * 1024
F32 = jnp.float32
BF16 = jnp.bfloat16
NT = (((1,), (1,)), ((), ()))
RIGHT = [(0, 1), (1, 2), (2, 3)]
LEFT = [(1, 0), (2, 1), (3, 2)]


def hop(x, chip_pairs):
    pairs = [(SLICES * a + c, SLICES * b + c) for a, b in chip_pairs for c in range(SLICES)]
    return lax.ppermute(x, "expert", pairs)


def swap(x):
    return lax.ppermute(x, "expert", [(i, i ^ 1) for i in range(lax.axis_size("expert"))])


def on_line():
    return lax.axis_size("expert") == LINE * SLICES


def slot_devices():
    devices = lax.axis_size("expert")
    if not on_line():
        return jnp.arange(devices)
    me = lax.axis_index("expert")
    chip, core = me // SLICES, me % SLICES
    chips = (chip - jnp.arange(LINE)) % LINE
    return jnp.concatenate([chips * SLICES + core, chips * SLICES + 1 - core])


def gather_rows(x):
    if not on_line():
        rows = lax.all_gather(x, "expert", axis=0, tiled=True)
        half = rows.shape[0] // 2
        return rows[:half], rows[half:]
    chip = lax.axis_index("expert") // SLICES
    right1 = hop(x, RIGHT)
    left1 = hop(x, LEFT)
    right2 = hop(right1, [(1, 2), (2, 3)])
    left2 = hop(left1, [(2, 1), (1, 0)])
    two = jnp.where(chip >= 2, right2, left2)
    far = hop(two, [(2, 3), (1, 0)])
    one = jnp.where(chip >= 1, right1, far)
    three = jnp.where(chip >= 3, far, left1)
    mine = jnp.concatenate([x, one, two, three], axis=0)
    return mine, swap(mine)


def scatter_sum(mine, other, residual):
    rows = residual.shape[0]
    if not on_line():
        total = lax.psum_scatter(
            jnp.concatenate([mine, other], axis=0), "expert", scatter_dimension=0, tiled=True
        )
        return (residual.astype(F32) + total.astype(F32)).astype(BF16)
    chip = lax.axis_index("expert") // SLICES
    part = (mine + swap(other)).reshape(LINE, rows, residual.shape[1])
    far = hop(jnp.where(chip < 2, part[1], part[3]), [(0, 1), (3, 2)])
    edge = hop(part[2], [(0, 1), (3, 2)])
    middle = hop(part[2] + far, [(1, 2), (2, 1)])
    right = hop(part[3] + jnp.where(chip == 1, edge, middle), RIGHT)
    left = hop(part[1] + jnp.where(chip == 2, edge, middle), LEFT)
    total = part[0].astype(F32) + right.astype(F32) + left.astype(F32)
    return (residual.astype(F32) + total).astype(BF16)


def stacked(a_ref, b_ref):
    return jnp.concatenate([a_ref[...], b_ref[...]], axis=0)


def split_store(value, a_ref, b_ref):
    half = a_ref.shape[0]
    a_ref[...] = value[:half].astype(a_ref.dtype)
    b_ref[...] = value[half:].astype(b_ref.dtype)


def forward_kernel(tiles, xm, xo, gate, wg, wu, wd, om, oo, acc_gate, acc_up, hidden):
    step = pl.program_id(0)

    @pl.when(step == 0)
    def _():
        acc_gate[...] = jnp.zeros_like(acc_gate)
        acc_up[...] = jnp.zeros_like(acc_up)

    @pl.when(step < tiles)
    def _():
        x = stacked(xm, xo)
        acc_gate[...] += jnp.dot(x, wg[...], preferred_element_type=F32)
        acc_up[...] += jnp.dot(x, wu[...], preferred_element_type=F32)

    @pl.when(step == tiles - 1)
    def _():
        pre = acc_gate[...]
        value = pre * jax.nn.sigmoid(pre) * acc_up[...] * gate[...]
        hidden[...] = value.astype(BF16)

    @pl.when(step >= tiles)
    def _():
        split_store(jnp.dot(hidden[...], wd[...], preferred_element_type=F32), om, oo)


def pre_kernel(tiles, xm, xo, wg, wu, pre_gate, pre_up):
    step = pl.program_id(0)
    x = stacked(xm, xo)

    @pl.when(step == 0)
    def _():
        pre_gate[...] = jnp.zeros_like(pre_gate)
        pre_up[...] = jnp.zeros_like(pre_up)

    pre_gate[...] += jnp.dot(x, wg[...], preferred_element_type=F32)
    pre_up[...] += jnp.dot(x, wu[...], preferred_element_type=F32)


def backward_kernel(
    tiles, gm, go, gate, pre_gate, pre_up, wd, wg, wu, om, oo, acc, d_gate, d_up
):
    step = pl.program_id(0)

    @pl.when(step == 0)
    def _():
        acc[...] = jnp.zeros_like(acc)

    @pl.when(step < tiles)
    def _():
        acc[...] += lax.dot_general(stacked(gm, go), wd[...], NT, preferred_element_type=F32)

    @pl.when(step == tiles - 1)
    def _():
        d_hidden = acc[...] * gate[...]
        pre = pre_gate[...]
        sig = jax.nn.sigmoid(pre)
        d_up[...] = (d_hidden * pre * sig).astype(BF16)
        d_gate[...] = (d_hidden * pre_up[...] * sig * (1.0 + pre * (1.0 - sig))).astype(BF16)

    @pl.when(step >= tiles)
    def _():
        value = lax.dot_general(d_gate[...], wg[...], NT, preferred_element_type=F32)
        value += lax.dot_general(d_up[...], wu[...], NT, preferred_element_type=F32)
        split_store(value, om, oo)


def specs(half, width, hid, tiles):
    first = lambda i: jnp.minimum(i, tiles - 1)
    second = lambda i: jnp.maximum(i - tiles, 0)
    return {
        "x": pl.BlockSpec((half, TILE), lambda i: (0, first(i))),
        "col1": pl.BlockSpec((TILE, hid), lambda i: (first(i), 0)),
        "col2": pl.BlockSpec((TILE, hid), lambda i: (second(i), 0)),
        "row1": pl.BlockSpec((hid, TILE), lambda i: (0, first(i))),
        "row2": pl.BlockSpec((hid, TILE), lambda i: (0, second(i))),
        "out": pl.BlockSpec((half, TILE), lambda i: (0, second(i))),
        "gate": pl.BlockSpec((2 * half, 1), lambda i: (0, 0)),
        "pre": pl.BlockSpec((2 * half, hid), lambda i: (0, 0)),
    }


def params():
    return pltpu.CompilerParams(vmem_limit_bytes=VMEM_LIMIT)


def cost(dots, half, width, hid, passes):
    return pl.CostEstimate(
        flops=2 * dots * 2 * half * width * hid,
        bytes_accessed=2 * width * (passes * hid + 4 * half),
        transcendentals=2 * half * hid,
    )


def forward_piece(xm, xo, gate, wg, wu, wd):
    half, width = xm.shape
    hid = wg.shape[1]
    tiles = width // TILE
    s = specs(half, width, hid, tiles)
    return pl.pallas_call(
        lambda *refs: forward_kernel(tiles, *refs),
        grid=(2 * tiles,),
        in_specs=[s["x"], s["x"], s["gate"], s["col1"], s["col1"], s["row2"]],
        out_specs=[s["out"], s["out"]],
        out_shape=[jax.ShapeDtypeStruct((half, width), BF16)] * 2,
        scratch_shapes=[
            pltpu.VMEM((2 * half, hid), F32),
            pltpu.VMEM((2 * half, hid), F32),
            pltpu.VMEM((2 * half, hid), BF16),
        ],
        compiler_params=params(),
        cost_estimate=cost(3, half, width, hid, 3),
        name="forward_piece",
    )(xm, xo, gate, wg, wu, wd)


def pre_piece(xm, xo, wg, wu):
    half, width = xm.shape
    hid = wg.shape[1]
    tiles = width // TILE
    s = specs(half, width, hid, tiles)
    return pl.pallas_call(
        lambda *refs: pre_kernel(tiles, *refs),
        grid=(tiles,),
        in_specs=[s["x"], s["x"], s["col1"], s["col1"]],
        out_specs=[s["pre"], s["pre"]],
        out_shape=[jax.ShapeDtypeStruct((2 * half, hid), F32)] * 2,
        compiler_params=params(),
        cost_estimate=cost(2, half, width, hid, 2),
        name="pre_piece",
    )(xm, xo, wg, wu)


def backward_piece(gm, go, gate, pre_gate, pre_up, wg, wu, wd):
    half, width = gm.shape
    hid = wg.shape[1]
    tiles = width // TILE
    s = specs(half, width, hid, tiles)
    return pl.pallas_call(
        lambda *refs: backward_kernel(tiles, *refs),
        grid=(2 * tiles,),
        in_specs=[s["x"], s["x"], s["gate"], s["pre"], s["pre"], s["row1"], s["col2"], s["col2"]],
        out_specs=[s["out"], s["out"]],
        out_shape=[jax.ShapeDtypeStruct((half, width), BF16)] * 2,
        scratch_shapes=[
            pltpu.VMEM((2 * half, hid), F32),
            pltpu.VMEM((2 * half, hid), BF16),
            pltpu.VMEM((2 * half, hid), BF16),
        ],
        compiler_params=params(),
        cost_estimate=cost(3, half, width, hid, 3),
        name="backward_piece",
    )(gm, go, gate, pre_gate, pre_up, wd, wg, wu)


def expert_gates(route_ids, gate_levels, token_counts):
    section = lax.axis_index("section")
    sections = lax.axis_size("section")
    devices = lax.axis_size("expert")
    experts = devices // SLICES
    routes, levels = route_ids[:, 0], gate_levels[:, 0].astype(F32)
    rows = routes.shape[2]
    ticks = jnp.arange(TICKS)
    batches = jnp.stack([ticks - section + sections - 1, ticks + section])
    counts = jnp.take_along_axis(token_counts[:, :, 0], batches, axis=1)
    live = jnp.arange(rows)[None, None, :] < counts[:, :, None]
    weights = levels / jnp.sum(levels, axis=-1, keepdims=True) * live[..., None].astype(F32)
    named = routes[..., None] == jnp.arange(experts)
    table = jnp.sum(jnp.where(named, weights[..., None], 0.0), axis=3)
    everyone = lax.all_gather(table, "expert", axis=0, tiled=False)
    expert = lax.axis_index("expert") // SLICES
    column = lax.dynamic_index_in_dim(everyone, expert, 4, keepdims=False)
    column = column[slot_devices()]
    return jnp.moveaxis(column, 0, 2).reshape(2, TICKS, devices * rows, 1)


def local(
    fwd_arriving,
    fwd_entering,
    bwd_arriving,
    bwd_entering,
    saved_inputs,
    w_gate,
    w_up,
    w_down,
    route_ids,
    gate_levels,
    token_counts,
):
    section = lax.axis_index("section")
    sections = lax.axis_size("section")
    wg, wu, wd = w_gate[0, 0], w_up[0, 0], w_down[0, 0]
    gates = expert_gates(route_ids, gate_levels, token_counts)
    ahead = [(i, (i + 1) % sections) for i in range(sections)]
    back = [(i, (i - 1) % sections) for i in range(sections)]
    fwd_state, bwd_state = fwd_arriving[0], bwd_arriving[0]
    fwd_list, bwd_list = [], []
    for tick in range(TICKS):
        fm, fo = gather_rows(fwd_state)
        sm, so = gather_rows(saved_inputs[0, tick])
        gm, go = gather_rows(bwd_state)
        fwd_out = forward_piece(fm, fo, gates[0, tick], wg, wu, wd)
        pre_gate, pre_up = pre_piece(sm, so, wg, wu)
        bwd_out = backward_piece(gm, go, gates[1, tick], pre_gate, pre_up, wg, wu, wd)
        fwd_state = scatter_sum(*fwd_out, fwd_state)
        bwd_state = scatter_sum(*bwd_out, bwd_state)
        fwd_list.append(fwd_state)
        bwd_list.append(bwd_state)
        if tick + 1 < TICKS:
            fwd_state = lax.ppermute(
                jnp.where(section == sections - 1, fwd_entering[tick], fwd_state), "section", ahead
            )
            bwd_state = lax.ppermute(
                jnp.where(section == 0, bwd_entering[tick], bwd_state), "section", back
            )
    return jnp.stack(fwd_list)[None], jnp.stack(bwd_list)[None]


def solution(mesh):
    return jax.shard_map(
        local,
        mesh=mesh,
        in_specs=(
            P("section", "expert", None),
            P(None, "expert", None),
            P("section", "expert", None),
            P(None, "expert", None),
            P("section", None, "expert", None),
            P("section", "expert", None, None),
            P("section", "expert", None, None),
            P("section", "expert", None, None),
            P(None, "section", None, "expert", None),
            P(None, "section", None, "expert", None),
            P(None, None, "expert"),
        ),
        out_specs=(P("section", None, "expert", None), P("section", None, "expert", None)),
        check_vma=False,
    )
```

```python
import jax
import jax.numpy as jnp
from jax import lax
from jax.experimental import pallas as pl
from jax.experimental.pallas import tpu as pltpu
from jax.sharding import PartitionSpec as P

SLICES = 2
TICKS = 2
TOPK = 2
LINE = 4
LANES = 128
TILE = 1024
AHEAD = 6
VMEM_LIMIT = 48 * 1024 * 1024
F32 = jnp.float32
BF16 = jnp.bfloat16
NT = (((1,), (1,)), ((), ()))
TN = (((0,), (0,)), ((), ()))


def on_line():
    return lax.axis_size("expert") == LINE * SLICES


def hop(x, step):
    devices = lax.axis_size("expert")
    return lax.ppermute(x, "expert", [(i, i ^ (SLICES * step)) for i in range(devices)])


def swap(x):
    return lax.ppermute(x, "expert", [(i, i ^ 1) for i in range(lax.axis_size("expert"))])


def turned(x, turn):
    sections = lax.axis_size("section")
    return lax.ppermute(x, "section", [(i, (i + turn) % sections) for i in range(sections)])


def after(x, *others):
    return lax.optimization_barrier((x, *others))[0] if others else x


def beside(results, *others):
    return list(lax.optimization_barrier((*results, *others)))[: len(results)] if others else list(results)


def capacity_of(rows):
    experts = lax.axis_size("expert") // SLICES
    return min(rows, 3 * rows * TOPK // (2 * experts))


def slot_tables(table):
    mine = jnp.concatenate([table] + [hop(table, k) for k in range(1, LINE)], axis=0)
    both = jnp.concatenate([mine, swap(mine)], axis=0)
    return both.reshape(SLICES * LINE, *table.shape)


def picks_of(levels, capacity):
    named = levels > 0
    place = jnp.cumsum(named.astype(jnp.int32), axis=-1) - 1
    places = jnp.arange(capacity)[:, None]
    return (named[..., None, :] & (place[..., None, :] == places)).astype(F32)


def gates_of_slots(table, everyone_here):
    rows = table.shape[0]
    capacity = capacity_of(rows)
    chip = lax.axis_index("expert") // SLICES
    experts = lax.axis_size("expert") // SLICES
    ways = 2 * TICKS
    levels = everyone_here[:, :, : ways * experts].astype(F32)
    levels = levels.reshape(SLICES * LINE, rows, ways, experts).transpose(2, 3, 0, 1)
    sums = jnp.maximum(jnp.sum(levels, axis=1), 1.0)
    is_mine = (jnp.arange(experts) == chip)[None, :, None, None]
    here = jnp.sum(jnp.where(is_mine, levels, 0.0), axis=1)
    gates = here / sums
    packed = jnp.sum(picks_of(here, capacity) * gates[:, :, None, :], axis=-1)
    pad = jnp.zeros((ways, slot_rows(rows) - rows - (LINE - 1) * capacity), F32)
    column = []
    for core in range(SLICES):
        at = core * LINE
        column += [gates[:, at], *[packed[:, at + k] for k in range(1, LINE)], pad]
    column = jnp.concatenate(column, axis=1)[:, :, None]
    return [[column[d * TICKS + t] for t in range(TICKS)] for d in range(2)]


def picks_away(table):
    rows = table.shape[0]
    chip = lax.axis_index("expert") // SLICES
    experts = lax.axis_size("expert") // SLICES
    own = table[:, : 2 * TICKS * experts].astype(F32).reshape(rows, 2 * TICKS, experts)
    chosen = (jnp.arange(experts)[None, :] == (chip ^ jnp.arange(1, LINE))[:, None]).astype(F32)
    away = jnp.sum(own[:, :, None] * chosen, axis=3).transpose(1, 2, 0)
    picks = picks_of(away, capacity_of(rows)).astype(BF16)
    return [[picks[d * TICKS + t] for t in range(TICKS)] for d in range(2)]


def slot_rows(rows):
    return -(-(rows + (LINE - 1) * capacity_of(rows)) // 16) * 16


def in_kernel(body, args, shapes, name):
    vmem = pl.BlockSpec(memory_space=pltpu.VMEM)
    return pl.pallas_call(
        body,
        in_specs=[vmem] * len(args),
        out_specs=[vmem] * len(shapes),
        out_shape=[pltpu.VMEM(shape, BF16) for shape in shapes],
        compiler_params=pltpu.CompilerParams(vmem_limit_bytes=VMEM_LIMIT // 4),
        cost_estimate=pl.CostEstimate(flops=0, bytes_accessed=0, transcendentals=0),
        name=name,
    )(*args)


def pack_kernel(x, picks, *outs):
    for i, out in enumerate(outs):
        for span in tiles(x.shape[1]):
            value = jnp.dot(picks[i], x[:, span], preferred_element_type=F32)
            out[:, span] = value.astype(BF16)


def join_kernel(*refs):
    blocks, out = refs[:-1], refs[-1]
    rows = sum(b.shape[0] for b in blocks)
    for span in tiles(out.shape[1]):
        parts = [b[:, span].astype(F32) for b in blocks]
        parts.append(jnp.zeros((out.shape[0] - rows, parts[0].shape[1]), F32))
        out[:, span] = jnp.concatenate(parts, axis=0).astype(BF16)


class Gather:
    def __init__(self, x, picks, *ready):
        self.own = x
        shape = (picks.shape[1], x.shape[1])
        packed = in_kernel(pack_kernel, [x, picks], [shape] * (LINE - 1), "pack")
        self.arrived = [hop(p, k + 1) for k, p in enumerate(beside(packed, *ready))]

    def blocks(self, *ready):
        rows, width = self.own.shape
        arrived = beside(self.arrived, *ready)
        (mine,) = in_kernel(join_kernel, [self.own, *arrived], [(slot_rows(rows), width)], "join")
        return [mine, swap(mine)]


class Give:
    def __init__(self, parts, residual, picks):
        self.residual, self.picks = residual, picks
        rows, capacity = residual.shape[0], picks.shape[1]
        part = parts[0] + swap(parts[1])
        self.own = part[:rows]
        starts = [rows + k * capacity for k in range(LINE - 1)]
        self.arrived = [hop(part[at : at + capacity], k + 1) for k, at in enumerate(starts)]

    def total(self, *ready):
        total = self.residual.astype(F32) + self.own.astype(F32)
        for pick, part in zip(self.picks, beside(self.arrived, *ready)):
            total += lax.dot_general(pick, part, TN, preferred_element_type=F32)
        return total.astype(BF16)


def silu_parts(pre):
    sig = jax.nn.sigmoid(pre)
    return sig, pre * sig


def backward_factors(pre_gate, pre_up, d_hidden):
    sig, silu = silu_parts(pre_gate)
    d_up = (d_hidden * silu).astype(BF16)
    d_gate = (d_hidden * pre_up * sig * (1.0 + pre_gate * (1.0 - sig))).astype(BF16)
    return d_gate, d_up


def tiles(width):
    tile = TILE if width % TILE == 0 else width
    return [slice(i, i + tile) for i in range(0, width, tile)]


class Stream:
    def __init__(self, groups):
        self.groups = list(groups)
        self.queue = [copy for group in self.groups for copy in group]
        self.start(AHEAD)

    def start(self, count):
        for copy in self.queue[:count]:
            copy.start()
        self.queue = self.queue[count:]

    def take(self):
        group = self.groups.pop(0)
        for copy in group:
            copy.wait()
        self.start(len(group))


def copies(src, dst, sems, axis):
    spans = tiles(src.shape[axis])
    at = (lambda s: (s, slice(None))) if axis == 0 else (lambda s: (slice(None), s))
    return [pltpu.make_async_copy(src.at[at(s)], dst.at[at(s)], sems.at[i]) for i, s in enumerate(spans)]


def rows_in(blocks, x, sems):
    r = blocks[0].shape[0]
    done = [
        pltpu.make_async_copy(b.at[:, : x.shape[1]], x.at[i * r : (i + 1) * r], sems.at[i])
        for i, b in enumerate(blocks)
    ]
    for copy in done:
        copy.start()
    return done


def split_store(value, outs, span):
    r = outs[0].shape[0]
    for i, o in enumerate(outs):
        o[:, span] = value[i * r : (i + 1) * r].astype(BF16)


def forward_kernel(n, *refs):
    blocks, (gate, wg, wu, wd), outs = refs[:n], refs[n : n + 4], refs[n + 4 : 2 * n + 4]
    x, g, u, d, acc_gate, acc_up, s_in, s_g, s_u, s_d = refs[2 * n + 4 :]
    arriving = rows_in(blocks, x, s_in)
    pairs = [list(p) for p in zip(copies(wg, g, s_g, 0), copies(wu, u, s_u, 0))]
    stream = Stream(pairs + [[c] for c in copies(wd, d, s_d, 1)])
    for copy in arriving:
        copy.wait()
    for i, span in enumerate(tiles(g.shape[0])):
        stream.take()
        for w, acc in ((g, acc_gate), (u, acc_up)):
            value = jnp.dot(x[:, span], w[span, :], preferred_element_type=F32)
            acc[...] = value if i == 0 else acc[...] + value
    hidden = (silu_parts(acc_gate[...])[1] * gate[...] * acc_up[...]).astype(BF16)
    for span in tiles(d.shape[1]):
        stream.take()
        split_store(jnp.dot(hidden, d[:, span], preferred_element_type=F32), outs, span)


def pre_kernel(n, *refs):
    blocks, (wg, wu, pre_gate, pre_up) = refs[:n], refs[n : n + 4]
    x, g, u, s_in, s_g, s_u = refs[n + 4 :]
    arriving = rows_in(blocks, x, s_in)
    pairs = [list(p) for p in zip(copies(wg, g, s_g, 0), copies(wu, u, s_u, 0))]
    stream = Stream(pairs)
    for copy in arriving:
        copy.wait()
    for i, span in enumerate(tiles(g.shape[0])):
        stream.take()
        for w, acc in ((g, pre_gate), (u, pre_up)):
            value = jnp.dot(x[:, span], w[span, :], preferred_element_type=F32)
            acc[...] = value if i == 0 else acc[...] + value


def backward_kernel(n, *refs):
    blocks, (gate, pre_gate, pre_up, wg, wu, wd) = refs[:n], refs[n : n + 6]
    outs = refs[n + 6 : 2 * n + 6]
    x, g, u, d, acc, s_in, s_g, s_u, s_d = refs[2 * n + 6 :]
    arriving = rows_in(blocks, x, s_in)
    pairs = [list(p) for p in zip(copies(wg, g, s_g, 0), copies(wu, u, s_u, 0))]
    stream = Stream([[c] for c in copies(wd, d, s_d, 1)] + pairs)
    for copy in arriving:
        copy.wait()
    for i, span in enumerate(tiles(d.shape[1])):
        stream.take()
        value = lax.dot_general(x[:, span], d[:, span], NT, preferred_element_type=F32)
        acc[...] = value if i == 0 else acc[...] + value
    d_gate, d_up = backward_factors(pre_gate[...], pre_up[...], acc[...] * gate[...])
    for span in tiles(g.shape[0]):
        stream.take()
        value = lax.dot_general(d_gate, g[span, :], NT, preferred_element_type=F32)
        value += lax.dot_general(d_up, u[span, :], NT, preferred_element_type=F32)
        split_store(value, outs, span)


def call(kernel, n, args, in_vmem, out_shape, scratch, dots, name):
    anywhere, vmem = pl.BlockSpec(memory_space=pl.ANY), pl.BlockSpec(memory_space=pltpu.VMEM)
    weight = args[-1].size
    return pl.pallas_call(
        lambda *refs: kernel(n, *refs),
        in_specs=[vmem if i in in_vmem else anywhere for i in range(len(args))],
        out_specs=[pl.BlockSpec(memory_space=o.memory_space) for o in out_shape],
        out_shape=out_shape,
        scratch_shapes=scratch,
        compiler_params=pltpu.CompilerParams(vmem_limit_bytes=VMEM_LIMIT),
        cost_estimate=pl.CostEstimate(
            flops=0,
            bytes_accessed=0,
            transcendentals=0,
        ),
        name=name,
    )(*args)


def scratch_of(rows, weights, accs, n):
    width, hid = weights[0].shape
    dma = pltpu.SemaphoreType.DMA
    buffers = [pltpu.VMEM((rows, width), BF16)] + [pltpu.VMEM(w.shape, BF16) for w in weights]
    buffers += [pltpu.VMEM((rows, hid), F32)] * accs
    return buffers + [dma((n,))] + [dma((len(tiles(width)),)) for _ in weights]


def forward_piece(blocks, gate, wg, wu, wd):
    n, r, width = len(blocks), blocks[0].shape[0], wg.shape[0]
    return call(
        forward_kernel,
        n,
        [*blocks, gate, wg, wu, wd],
        (n,),
        [pltpu.VMEM((r, width), BF16)] * n,
        scratch_of(n * r, (wg, wu, wd), 2, n),
        3,
        "forward_piece",
    )


def pre_piece(blocks, wg, wu):
    n, r = len(blocks), blocks[0].shape[0]
    shape = pltpu.VMEM((n * r, wg.shape[1]), F32)
    scratch = scratch_of(n * r, (wg, wu), 0, n)
    return call(pre_kernel, n, [*blocks, wg, wu], (), [shape, shape], scratch, 2, "pre_piece")


def backward_piece(blocks, gate, pre, wg, wu, wd):
    n, r, width = len(blocks), blocks[0].shape[0], wg.shape[0]
    return call(
        backward_kernel,
        n,
        [*blocks, gate, *pre, wg, wu, wd],
        (n, n + 1, n + 2),
        [pltpu.VMEM((r, width), BF16)] * n,
        scratch_of(n * r, (wg, wu, wd), 1, n),
        3,
        "backward_piece",
    )


def level_table(route_ids, gate_levels, token_counts):
    section = lax.axis_index("section")
    sections = lax.axis_size("section")
    experts = lax.axis_size("expert") // SLICES
    routes, levels = route_ids[:, 0], gate_levels[:, 0]
    rows = routes.shape[2]
    first = lambda d, at: lax.dynamic_slice(token_counts[d, :, 0], (at,), (TICKS,))
    counts = jnp.stack([first(0, sections - 1 - section), first(1, section)])
    live = jnp.arange(rows)[None, None, :] < counts[:, :, None]
    named = (routes[..., None] == jnp.arange(experts)) & live[..., None, None]
    table = jnp.sum(jnp.where(named, levels[..., None], 0), axis=3)
    table = jnp.moveaxis(table, 2, 0).reshape(rows, -1).astype(BF16)
    return jnp.pad(table, ((0, 0), (0, -table.shape[1] % LANES)))


def gates_of(tables):
    devices = lax.axis_size("expert")
    experts = devices // SLICES
    mine = lax.axis_index("expert") // SLICES
    levels = tables[:, : 2 * TICKS * experts].astype(F32).reshape(-1, 2 * TICKS, experts)
    sums = jnp.maximum(jnp.sum(levels, axis=2), 1.0)
    own = jnp.sum(jnp.where(jnp.arange(experts) == mine, levels, 0.0), axis=2)
    gates = own / sums
    return [[gates[:, d * TICKS + t][:, None] for t in range(TICKS)] for d in range(2)]


def relay(x, entering, end, turn):
    return jnp.where(lax.axis_index("section") == end, entering, x), turn


def everyone(x):
    return lax.all_gather(x, "expert", axis=0, tiled=True)


def summed(parts, residual):
    parts = lax.psum_scatter(parts, "expert", scatter_dimension=0, tiled=True)
    return (residual.astype(F32) + parts.astype(F32)).astype(BF16)


def whole_line(fwd, bwd, saved, weights, tables, fwd_entering, bwd_entering):
    last = lax.axis_size("section") - 1
    (f_picks0, f_picks1), (b_picks0, b_picks1) = picks_away(tables)
    slots = slot_tables(tables)
    s0, g0 = Gather(saved[0], b_picks0, slots), Gather(bwd, b_picks0, slots)
    f_gates, b_gates = gates_of_slots(tables, slots)
    x0 = Gather(fwd, f_picks0, *s0.arrived)
    pre = pre_piece(s0.blocks(), *weights[:2])
    parts = backward_piece(g0.blocks(), b_gates[0], pre, *weights)
    parts = beside(parts, *x0.arrived)
    b0 = Give(parts, bwd, b_picks0)
    parts = forward_piece(x0.blocks(*parts), f_gates[0], *weights)
    f0 = Give(beside(parts, *b0.arrived), fwd, f_picks0)
    s1 = Gather(saved[1], b_picks1, *b0.arrived)
    b_out0 = b0.total()
    bwd1 = turned(*relay(b_out0, bwd_entering[0], 0, -1))
    g1 = Gather(bwd1, b_picks1, *f0.arrived)
    f_out0 = f0.total()
    fwd1 = turned(*relay(f_out0, fwd_entering[0], last, 1))
    pre = pre_piece(s1.blocks(fwd1), *weights[:2])
    x1 = Gather(fwd1, f_picks1, *s1.arrived)
    parts = backward_piece(g1.blocks(), b_gates[1], pre, *weights)
    parts = beside(parts, *x1.arrived)
    b1 = Give(parts, bwd1, b_picks1)
    parts = forward_piece(x1.blocks(*parts), f_gates[1], *weights)
    f1 = Give(beside(parts, *b1.arrived), fwd1, f_picks1)
    return [f_out0, f1.total()], [b_out0, b1.total()]


def plain(fwd, bwd, saved, weights, tables, fwd_entering, bwd_entering):
    wg, wu, wd = weights
    last = lax.axis_size("section") - 1

    def dot(a, b):
        return jnp.dot(a, b, preferred_element_type=F32)

    def dot_nt(a, b):
        return lax.dot_general(a, b, NT, preferred_element_type=F32)

    gates = gates_of(everyone(tables))
    fwd_list, bwd_list = [], []
    for tick in range(TICKS):
        x, s, g = everyone(fwd), everyone(saved[tick]), everyone(bwd)
        hidden = silu_parts(dot(x, wg))[1] * gates[0][tick] * dot(x, wu)
        fwd_list.append(summed(dot(hidden.astype(BF16), wd).astype(BF16), fwd))
        d_hidden = dot_nt(g, wd) * gates[1][tick]
        d_gate, d_up = backward_factors(dot(s, wg), dot(s, wu), d_hidden)
        back = dot_nt(d_gate, wg) + dot_nt(d_up, wu)
        bwd_list.append(summed(back.astype(BF16), bwd))
        if tick + 1 < TICKS:
            fwd = turned(*relay(fwd_list[-1], fwd_entering[tick], last, 1))
            bwd = turned(*relay(bwd_list[-1], bwd_entering[tick], 0, -1))
    return fwd_list, bwd_list


def local(
    fwd_arriving,
    fwd_entering,
    bwd_arriving,
    bwd_entering,
    saved_inputs,
    w_gate,
    w_up,
    w_down,
    route_ids,
    gate_levels,
    token_counts,
):
    run = whole_line if on_line() else plain
    fwd_list, bwd_list = run(
        fwd_arriving[0],
        bwd_arriving[0],
        saved_inputs[0],
        (w_gate[0, 0], w_up[0, 0], w_down[0, 0]),
        level_table(route_ids, gate_levels, token_counts),
        fwd_entering,
        bwd_entering,
    )
    return jnp.stack(fwd_list)[None], jnp.stack(bwd_list)[None]


def solution(mesh):
    return jax.shard_map(
        local,
        mesh=mesh,
        in_specs=(
            P("section", "expert", None),
            P(None, "expert", None),
            P("section", "expert", None),
            P(None, "expert", None),
            P("section", None, "expert", None),
            P("section", "expert", None, None),
            P("section", "expert", None, None),
            P("section", "expert", None, None),
            P(None, "section", None, "expert", None),
            P(None, "section", None, "expert", None),
            P(None, None, "expert"),
        ),
        out_specs=(P("section", None, "expert", None), P("section", None, "expert", None)),
        check_vma=False,
    )
```

```python
import jax
import jax.numpy as jnp
from jax import lax
from jax.experimental import pallas as pl
from jax.experimental.pallas import tpu as pltpu
from jax.sharding import PartitionSpec as P

SLICES = 2
TICKS = 2
TOPK = 2
LINE = 4
LANES = 128
TILE = 1024
AHEAD = 6
VMEM_LIMIT = 48 * 1024 * 1024
F32 = jnp.float32
BF16 = jnp.bfloat16
NT = (((1,), (1,)), ((), ()))
TN = (((0,), (0,)), ((), ()))


def on_line():
    return lax.axis_size("expert") == LINE * SLICES


def hop(x, step):
    devices = lax.axis_size("expert")
    return lax.ppermute(x, "expert", [(i, i ^ (SLICES * step)) for i in range(devices)])


def swap(x):
    return lax.ppermute(x, "expert", [(i, i ^ 1) for i in range(lax.axis_size("expert"))])


def turned(x, turn):
    sections = lax.axis_size("section")
    return lax.ppermute(x, "section", [(i, (i + turn) % sections) for i in range(sections)])


def after(x, *others):
    return lax.optimization_barrier((x, *others))[0] if others else x


def beside(results, *others):
    return list(lax.optimization_barrier((*results, *others)))[: len(results)] if others else list(results)


def capacity_of(rows):
    experts = lax.axis_size("expert") // SLICES
    return min(rows, 3 * rows * TOPK // (2 * experts))


def slot_tables(table):
    mine = jnp.concatenate([table] + [hop(table, k) for k in range(1, LINE)], axis=0)
    both = jnp.concatenate([mine, swap(mine)], axis=0)
    return both.reshape(SLICES * LINE, *table.shape)


def picks_of(levels, capacity):
    named = levels > 0
    place = jnp.cumsum(named.astype(jnp.int32), axis=-1) - 1
    places = jnp.arange(capacity)[:, None]
    return (named[..., None, :] & (place[..., None, :] == places)).astype(F32)


def gates_of_slots(table, everyone_here):
    rows = table.shape[0]
    capacity = capacity_of(rows)
    chip = lax.axis_index("expert") // SLICES
    experts = lax.axis_size("expert") // SLICES
    ways = 2 * TICKS
    levels = everyone_here[:, :, : ways * experts].astype(F32)
    levels = levels.reshape(SLICES * LINE, rows, ways, experts).transpose(2, 3, 0, 1)
    sums = jnp.maximum(jnp.sum(levels, axis=1), 1.0)
    is_mine = (jnp.arange(experts) == chip)[None, :, None, None]
    here = jnp.sum(jnp.where(is_mine, levels, 0.0), axis=1)
    gates = here / sums
    packed = jnp.sum(picks_of(here, capacity) * gates[:, :, None, :], axis=-1)
    pad = jnp.zeros((ways, slot_rows(rows) - rows - (LINE - 1) * capacity), F32)
    column = []
    for core in range(SLICES):
        at = core * LINE
        column += [gates[:, at], *[packed[:, at + k] for k in range(1, LINE)], pad]
    column = jnp.concatenate(column, axis=1)[:, :, None]
    return [[column[d * TICKS + t] for t in range(TICKS)] for d in range(2)]


def picks_away(table):
    rows = table.shape[0]
    chip = lax.axis_index("expert") // SLICES
    experts = lax.axis_size("expert") // SLICES
    own = table[:, : 2 * TICKS * experts].astype(F32).reshape(rows, 2 * TICKS, experts)
    chosen = (jnp.arange(experts)[None, :] == (chip ^ jnp.arange(1, LINE))[:, None]).astype(F32)
    away = jnp.sum(own[:, :, None] * chosen, axis=3).transpose(1, 2, 0)
    picks = picks_of(away, capacity_of(rows)).astype(BF16)
    return [[picks[d * TICKS + t] for t in range(TICKS)] for d in range(2)]


def slot_rows(rows):
    return -(-(rows + (LINE - 1) * capacity_of(rows)) // 16) * 16


def in_kernel(body, args, shapes, name):
    vmem = pl.BlockSpec(memory_space=pltpu.VMEM)
    return pl.pallas_call(
        body,
        in_specs=[vmem] * len(args),
        out_specs=[vmem] * len(shapes),
        out_shape=[pltpu.VMEM(shape, BF16) for shape in shapes],
        compiler_params=pltpu.CompilerParams(vmem_limit_bytes=VMEM_LIMIT // 4),
        cost_estimate=pl.CostEstimate(flops=0, bytes_accessed=0, transcendentals=0),
        name=name,
    )(*args)


def pack_kernel(x, picks, *outs):
    for i, out in enumerate(outs):
        for span in tiles(x.shape[1]):
            value = jnp.dot(picks[i], x[:, span], preferred_element_type=F32)
            out[:, span] = value.astype(BF16)


def join_kernel(*refs):
    blocks, out = refs[:-1], refs[-1]
    rows = sum(b.shape[0] for b in blocks)
    for span in tiles(out.shape[1]):
        parts = [b[:, span].astype(F32) for b in blocks]
        parts.append(jnp.zeros((out.shape[0] - rows, parts[0].shape[1]), F32))
        out[:, span] = jnp.concatenate(parts, axis=0).astype(BF16)


def add_kernel(a, b, *outs):
    for span in tiles(a.shape[1]):
        value = a[:, span].astype(F32) + b[:, span].astype(F32)
        at = 0
        for out in outs:
            out[:, span] = value[at : at + out.shape[0]].astype(BF16)
            at += out.shape[0]


class Gather:
    def __init__(self, x, picks, *ready):
        self.own = x
        shape = (picks.shape[1], x.shape[1])
        packed = in_kernel(pack_kernel, [x, after(picks, *ready)], [shape] * (LINE - 1), "pack")
        self.arrived = [hop(p, k + 1) for k, p in enumerate(packed)]

    def blocks(self, *ready):
        rows, width = self.own.shape
        arrived = beside(self.arrived, *ready)
        (mine,) = in_kernel(join_kernel, [self.own, *arrived], [(slot_rows(rows), width)], "join")
        return [mine, swap(mine)]


class Give:
    def __init__(self, parts, residual, picks):
        self.residual, self.picks = residual, picks
        capacity = picks.shape[1]
        shapes = [residual.shape] + [(capacity, residual.shape[1])] * (LINE - 1)
        self.own, *away = in_kernel(add_kernel, [parts[0], swap(parts[1])], shapes, "add")
        self.arrived = [hop(part, k + 1) for k, part in enumerate(away)]

    def total(self, *ready):
        total = self.residual.astype(F32) + self.own.astype(F32)
        for pick, part in zip(self.picks, beside(self.arrived, *ready)):
            total += lax.dot_general(pick, part, TN, preferred_element_type=F32)
        return total.astype(BF16)


def silu_parts(pre):
    sig = jax.nn.sigmoid(pre)
    return sig, pre * sig


def backward_factors(pre_gate, pre_up, d_hidden):
    sig, silu = silu_parts(pre_gate)
    d_up = (d_hidden * silu).astype(BF16)
    d_gate = (d_hidden * pre_up * sig * (1.0 + pre_gate * (1.0 - sig))).astype(BF16)
    return d_gate, d_up


def tiles(width):
    tile = TILE if width % TILE == 0 else width
    return [slice(i, i + tile) for i in range(0, width, tile)]


class Stream:
    def __init__(self, groups):
        self.groups = list(groups)
        self.queue = [copy for group in self.groups for copy in group]
        self.start(AHEAD)

    def start(self, count):
        for copy in self.queue[:count]:
            copy.start()
        self.queue = self.queue[count:]

    def take(self):
        group = self.groups.pop(0)
        for copy in group:
            copy.wait()
        self.start(len(group))


def copies(src, dst, sems, axis):
    spans = tiles(src.shape[axis])
    at = (lambda s: (s, slice(None))) if axis == 0 else (lambda s: (slice(None), s))
    return [pltpu.make_async_copy(src.at[at(s)], dst.at[at(s)], sems.at[i]) for i, s in enumerate(spans)]


def rows_in(blocks, x, sems):
    r = blocks[0].shape[0]
    done = [
        pltpu.make_async_copy(b.at[:, : x.shape[1]], x.at[i * r : (i + 1) * r], sems.at[i])
        for i, b in enumerate(blocks)
    ]
    for copy in done:
        copy.start()
    return done


def split_store(value, outs, span):
    r = outs[0].shape[0]
    for i, o in enumerate(outs):
        o[:, span] = value[i * r : (i + 1) * r].astype(BF16)


def forward_kernel(n, *refs):
    blocks, (gate, wg, wu, wd), outs = refs[:n], refs[n : n + 4], refs[n + 4 : 2 * n + 4]
    x, g, u, d, acc_gate, acc_up, s_in, s_g, s_u, s_d = refs[2 * n + 4 :]
    arriving = rows_in(blocks, x, s_in)
    pairs = [list(p) for p in zip(copies(wg, g, s_g, 0), copies(wu, u, s_u, 0))]
    stream = Stream(pairs + [[c] for c in copies(wd, d, s_d, 1)])
    for copy in arriving:
        copy.wait()
    for i, span in enumerate(tiles(g.shape[0])):
        stream.take()
        for w, acc in ((g, acc_gate), (u, acc_up)):
            value = jnp.dot(x[:, span], w[span, :], preferred_element_type=F32)
            acc[...] = value if i == 0 else acc[...] + value
    hidden = (silu_parts(acc_gate[...])[1] * gate[...] * acc_up[...]).astype(BF16)
    for span in tiles(d.shape[1]):
        stream.take()
        split_store(jnp.dot(hidden, d[:, span], preferred_element_type=F32), outs, span)


def pre_kernel(n, *refs):
    blocks, (wg, wu, pre_gate, pre_up) = refs[:n], refs[n : n + 4]
    x, g, u, s_in, s_g, s_u = refs[n + 4 :]
    arriving = rows_in(blocks, x, s_in)
    pairs = [list(p) for p in zip(copies(wg, g, s_g, 0), copies(wu, u, s_u, 0))]
    stream = Stream(pairs)
    for copy in arriving:
        copy.wait()
    for i, span in enumerate(tiles(g.shape[0])):
        stream.take()
        for w, acc in ((g, pre_gate), (u, pre_up)):
            value = jnp.dot(x[:, span], w[span, :], preferred_element_type=F32)
            acc[...] = value if i == 0 else acc[...] + value


def backward_kernel(n, *refs):
    blocks, (gate, pre_gate, pre_up, wg, wu, wd) = refs[:n], refs[n : n + 6]
    outs = refs[n + 6 : 2 * n + 6]
    x, g, u, d, acc, s_in, s_g, s_u, s_d = refs[2 * n + 6 :]
    arriving = rows_in(blocks, x, s_in)
    pairs = [list(p) for p in zip(copies(wg, g, s_g, 0), copies(wu, u, s_u, 0))]
    stream = Stream([[c] for c in copies(wd, d, s_d, 1)] + pairs)
    for copy in arriving:
        copy.wait()
    for i, span in enumerate(tiles(d.shape[1])):
        stream.take()
        value = lax.dot_general(x[:, span], d[:, span], NT, preferred_element_type=F32)
        acc[...] = value if i == 0 else acc[...] + value
    d_gate, d_up = backward_factors(pre_gate[...], pre_up[...], acc[...] * gate[...])
    for span in tiles(g.shape[0]):
        stream.take()
        value = lax.dot_general(d_gate, g[span, :], NT, preferred_element_type=F32)
        value += lax.dot_general(d_up, u[span, :], NT, preferred_element_type=F32)
        split_store(value, outs, span)


def call(kernel, n, args, in_vmem, out_shape, scratch, dots, name):
    anywhere, vmem = pl.BlockSpec(memory_space=pl.ANY), pl.BlockSpec(memory_space=pltpu.VMEM)
    weight = args[-1].size
    return pl.pallas_call(
        lambda *refs: kernel(n, *refs),
        in_specs=[vmem if i in in_vmem else anywhere for i in range(len(args))],
        out_specs=[pl.BlockSpec(memory_space=o.memory_space) for o in out_shape],
        out_shape=out_shape,
        scratch_shapes=scratch,
        compiler_params=pltpu.CompilerParams(vmem_limit_bytes=VMEM_LIMIT),
        cost_estimate=pl.CostEstimate(
            flops=0,
            bytes_accessed=0,
            transcendentals=0,
        ),
        name=name,
    )(*args)


def scratch_of(rows, weights, accs, n):
    width, hid = weights[0].shape
    dma = pltpu.SemaphoreType.DMA
    buffers = [pltpu.VMEM((rows, width), BF16)] + [pltpu.VMEM(w.shape, BF16) for w in weights]
    buffers += [pltpu.VMEM((rows, hid), F32)] * accs
    return buffers + [dma((n,))] + [dma((len(tiles(width)),)) for _ in weights]


def forward_piece(blocks, gate, wg, wu, wd):
    n, r, width = len(blocks), blocks[0].shape[0], wg.shape[0]
    return call(
        forward_kernel,
        n,
        [*blocks, gate, wg, wu, wd],
        (n,),
        [pltpu.VMEM((r, width), BF16)] * n,
        scratch_of(n * r, (wg, wu, wd), 2, n),
        3,
        "forward_piece",
    )


def pre_piece(blocks, wg, wu):
    n, r = len(blocks), blocks[0].shape[0]
    shape = pltpu.VMEM((n * r, wg.shape[1]), F32)
    scratch = scratch_of(n * r, (wg, wu), 0, n)
    return call(pre_kernel, n, [*blocks, wg, wu], (), [shape, shape], scratch, 2, "pre_piece")


def backward_piece(blocks, gate, pre, wg, wu, wd):
    n, r, width = len(blocks), blocks[0].shape[0], wg.shape[0]
    return call(
        backward_kernel,
        n,
        [*blocks, gate, *pre, wg, wu, wd],
        (n, n + 1, n + 2),
        [pltpu.VMEM((r, width), BF16)] * n,
        scratch_of(n * r, (wg, wu, wd), 1, n),
        3,
        "backward_piece",
    )


def level_table(route_ids, gate_levels, token_counts):
    section = lax.axis_index("section")
    sections = lax.axis_size("section")
    experts = lax.axis_size("expert") // SLICES
    routes, levels = route_ids[:, 0], gate_levels[:, 0]
    rows = routes.shape[2]
    first = lambda d, at: lax.dynamic_slice(token_counts[d, :, 0], (at,), (TICKS,))
    counts = jnp.stack([first(0, sections - 1 - section), first(1, section)])
    live = jnp.arange(rows)[None, None, :] < counts[:, :, None]
    named = (routes[..., None] == jnp.arange(experts)) & live[..., None, None]
    table = jnp.sum(jnp.where(named, levels[..., None], 0), axis=3)
    table = jnp.moveaxis(table, 2, 0).reshape(rows, -1).astype(BF16)
    return jnp.pad(table, ((0, 0), (0, -table.shape[1] % LANES)))


def gates_of(tables):
    devices = lax.axis_size("expert")
    experts = devices // SLICES
    mine = lax.axis_index("expert") // SLICES
    levels = tables[:, : 2 * TICKS * experts].astype(F32).reshape(-1, 2 * TICKS, experts)
    sums = jnp.maximum(jnp.sum(levels, axis=2), 1.0)
    own = jnp.sum(jnp.where(jnp.arange(experts) == mine, levels, 0.0), axis=2)
    gates = own / sums
    return [[gates[:, d * TICKS + t][:, None] for t in range(TICKS)] for d in range(2)]


def relay(x, entering, end, turn):
    return jnp.where(lax.axis_index("section") == end, entering, x), turn


def everyone(x):
    return lax.all_gather(x, "expert", axis=0, tiled=True)


def summed(parts, residual):
    parts = lax.psum_scatter(parts, "expert", scatter_dimension=0, tiled=True)
    return (residual.astype(F32) + parts.astype(F32)).astype(BF16)


def whole_line(fwd, bwd, saved, weights, tables, fwd_entering, bwd_entering):
    last = lax.axis_size("section") - 1
    (f_picks0, f_picks1), (b_picks0, b_picks1) = picks_away(tables)
    slots = slot_tables(tables)
    s0, g0 = Gather(saved[0], b_picks0, slots), Gather(bwd, b_picks0, slots)
    f_gates, b_gates = gates_of_slots(tables, slots)
    x0 = Gather(fwd, f_picks0, *s0.arrived)
    pre = pre_piece(s0.blocks(), *weights[:2])
    parts = backward_piece(g0.blocks(), b_gates[0], pre, *weights)
    parts = [*beside(parts[:1], *x0.arrived), parts[1]]
    b0 = Give(parts, bwd, b_picks0)
    parts = forward_piece(x0.blocks(*parts), f_gates[0], *weights)
    f0 = Give(beside(parts, *b0.arrived), fwd, f_picks0)
    s1 = Gather(saved[1], b_picks1, *x0.arrived)
    b_out0 = b0.total()
    bwd1 = turned(*relay(b_out0, bwd_entering[0], 0, -1))
    g1 = Gather(bwd1, b_picks1, *f0.arrived)
    f_out0 = f0.total()
    fwd1 = turned(*relay(f_out0, fwd_entering[0], last, 1))
    pre = pre_piece(s1.blocks(fwd1), *weights[:2])
    x1 = Gather(fwd1, f_picks1, *s1.arrived)
    parts = backward_piece(g1.blocks(), b_gates[1], pre, *weights)
    parts = [*beside(parts[:1], *x1.arrived), parts[1]]
    b1 = Give(parts, bwd1, b_picks1)
    parts = forward_piece(x1.blocks(*parts), f_gates[1], *weights)
    f1 = Give(beside(parts, *b1.arrived), fwd1, f_picks1)
    return [f_out0, f1.total()], [b_out0, b1.total()]


def plain(fwd, bwd, saved, weights, tables, fwd_entering, bwd_entering):
    wg, wu, wd = weights
    last = lax.axis_size("section") - 1

    def dot(a, b):
        return jnp.dot(a, b, preferred_element_type=F32)

    def dot_nt(a, b):
        return lax.dot_general(a, b, NT, preferred_element_type=F32)

    gates = gates_of(everyone(tables))
    fwd_list, bwd_list = [], []
    for tick in range(TICKS):
        x, s, g = everyone(fwd), everyone(saved[tick]), everyone(bwd)
        hidden = silu_parts(dot(x, wg))[1] * gates[0][tick] * dot(x, wu)
        fwd_list.append(summed(dot(hidden.astype(BF16), wd).astype(BF16), fwd))
        d_hidden = dot_nt(g, wd) * gates[1][tick]
        d_gate, d_up = backward_factors(dot(s, wg), dot(s, wu), d_hidden)
        back = dot_nt(d_gate, wg) + dot_nt(d_up, wu)
        bwd_list.append(summed(back.astype(BF16), bwd))
        if tick + 1 < TICKS:
            fwd = turned(*relay(fwd_list[-1], fwd_entering[tick], last, 1))
            bwd = turned(*relay(bwd_list[-1], bwd_entering[tick], 0, -1))
    return fwd_list, bwd_list


def local(
    fwd_arriving,
    fwd_entering,
    bwd_arriving,
    bwd_entering,
    saved_inputs,
    w_gate,
    w_up,
    w_down,
    route_ids,
    gate_levels,
    token_counts,
):
    run = whole_line if on_line() else plain
    fwd_list, bwd_list = run(
        fwd_arriving[0],
        bwd_arriving[0],
        saved_inputs[0],
        (w_gate[0, 0], w_up[0, 0], w_down[0, 0]),
        level_table(route_ids, gate_levels, token_counts),
        fwd_entering,
        bwd_entering,
    )
    return jnp.stack(fwd_list)[None], jnp.stack(bwd_list)[None]


def solution(mesh):
    return jax.shard_map(
        local,
        mesh=mesh,
        in_specs=(
            P("section", "expert", None),
            P(None, "expert", None),
            P("section", "expert", None),
            P(None, "expert", None),
            P("section", None, "expert", None),
            P("section", "expert", None, None),
            P("section", "expert", None, None),
            P("section", "expert", None, None),
            P(None, "section", None, "expert", None),
            P(None, "section", None, "expert", None),
            P(None, None, "expert"),
        ),
        out_specs=(P("section", None, "expert", None), P("section", None, "expert", None)),
        check_vma=False,
    )
```

```python
import jax
import jax.numpy as jnp
from jax import lax
from jax.experimental import pallas as pl
from jax.experimental.pallas import tpu as pltpu
from jax.sharding import PartitionSpec as P

SLICES = 2
TICKS = 2
TOPK = 2
LINE = 4
LANES = 128
TILE = 1024
AHEAD = 6
VMEM_LIMIT = 48 * 1024 * 1024
F32 = jnp.float32
BF16 = jnp.bfloat16
NT = (((1,), (1,)), ((), ()))
TN = (((0,), (0,)), ((), ()))


def on_line():
    return lax.axis_size("expert") == LINE * SLICES


def hop(x, step):
    devices = lax.axis_size("expert")
    return lax.ppermute(x, "expert", [(i, i ^ (SLICES * step)) for i in range(devices)])


def swap(x):
    return lax.ppermute(x, "expert", [(i, i ^ 1) for i in range(lax.axis_size("expert"))])


def turned(x, turn):
    sections = lax.axis_size("section")
    return lax.ppermute(x, "section", [(i, (i + turn) % sections) for i in range(sections)])


def after(x, *others):
    return lax.optimization_barrier((x, *others))[0] if others else x


def beside(results, *others):
    return list(lax.optimization_barrier((*results, *others)))[: len(results)] if others else list(results)


def capacity_of(rows):
    experts = lax.axis_size("expert") // SLICES
    return min(rows, 3 * rows * TOPK // (2 * experts))


def slot_tables(table):
    mine = jnp.concatenate([table] + [hop(table, k) for k in range(1, LINE)], axis=0)
    both = jnp.concatenate([mine, swap(mine)], axis=0)
    return both.reshape(SLICES * LINE, *table.shape)


def picks_of(levels, capacity):
    named = levels > 0
    place = jnp.cumsum(named.astype(jnp.int32), axis=-1) - 1
    places = jnp.arange(capacity)[:, None]
    return (named[..., None, :] & (place[..., None, :] == places)).astype(F32)


def gates_of_slots(table, everyone_here):
    rows = table.shape[0]
    capacity = capacity_of(rows)
    chip = lax.axis_index("expert") // SLICES
    experts = lax.axis_size("expert") // SLICES
    ways = 2 * TICKS
    levels = everyone_here[:, :, : ways * experts].astype(F32)
    levels = levels.reshape(SLICES * LINE, rows, ways, experts).transpose(2, 3, 0, 1)
    sums = jnp.maximum(jnp.sum(levels, axis=1), 1.0)
    is_mine = (jnp.arange(experts) == chip)[None, :, None, None]
    here = jnp.sum(jnp.where(is_mine, levels, 0.0), axis=1)
    gates = here / sums
    packed = jnp.sum(picks_of(here, capacity) * gates[:, :, None, :], axis=-1)
    pad = jnp.zeros((ways, slot_rows(rows) - rows - (LINE - 1) * capacity), F32)
    column = []
    for core in range(SLICES):
        at = core * LINE
        column += [gates[:, at], *[packed[:, at + k] for k in range(1, LINE)], pad]
    column = jnp.concatenate(column, axis=1)[:, :, None]
    return [[column[d * TICKS + t] for t in range(TICKS)] for d in range(2)]


def picks_away(table):
    rows = table.shape[0]
    chip = lax.axis_index("expert") // SLICES
    experts = lax.axis_size("expert") // SLICES
    own = table[:, : 2 * TICKS * experts].astype(F32).reshape(rows, 2 * TICKS, experts)
    chosen = (jnp.arange(experts)[None, :] == (chip ^ jnp.arange(1, LINE))[:, None]).astype(F32)
    away = jnp.sum(own[:, :, None] * chosen, axis=3).transpose(1, 2, 0)
    picks = picks_of(away, capacity_of(rows)).astype(BF16)
    return [[picks[d * TICKS + t] for t in range(TICKS)] for d in range(2)]


def slot_rows(rows):
    return -(-(rows + (LINE - 1) * capacity_of(rows)) // 16) * 16


def in_kernel(body, args, shapes, name):
    vmem = pl.BlockSpec(memory_space=pltpu.VMEM)
    return pl.pallas_call(
        body,
        in_specs=[vmem] * len(args),
        out_specs=[vmem] * len(shapes),
        out_shape=[pltpu.VMEM(shape, BF16) for shape in shapes],
        compiler_params=pltpu.CompilerParams(vmem_limit_bytes=VMEM_LIMIT // 4),
        cost_estimate=pl.CostEstimate(flops=0, bytes_accessed=0, transcendentals=0),
        name=name,
    )(*args)


def pack_kernel(x, picks, *outs):
    for i, out in enumerate(outs):
        for span in tiles(x.shape[1]):
            value = jnp.dot(picks[i], x[:, span], preferred_element_type=F32)
            out[:, span] = value.astype(BF16)


def join_kernel(*refs):
    blocks, out = refs[:-1], refs[-1]
    rows = sum(b.shape[0] for b in blocks)
    for span in tiles(out.shape[1]):
        parts = [b[:, span].astype(F32) for b in blocks]
        parts.append(jnp.zeros((out.shape[0] - rows, parts[0].shape[1]), F32))
        out[:, span] = jnp.concatenate(parts, axis=0).astype(BF16)


def add_kernel(a, b, *outs):
    for span in tiles(a.shape[1]):
        value = a[:, span].astype(F32) + b[:, span].astype(F32)
        at = 0
        for out in outs:
            out[:, span] = value[at : at + out.shape[0]].astype(BF16)
            at += out.shape[0]


class Gather:
    def __init__(self, x, picks, *ready):
        self.own = x
        shape = (picks.shape[1], x.shape[1])
        packed = in_kernel(pack_kernel, [x, after(picks, *ready)], [shape] * (LINE - 1), "pack")
        self.arrived = [hop(p, k + 1) for k, p in enumerate(packed)]

    def blocks(self, *ready):
        rows, width = self.own.shape
        arrived = beside(self.arrived, *ready)
        (mine,) = in_kernel(join_kernel, [self.own, *arrived], [(slot_rows(rows), width)], "join")
        return [mine, swap(mine)]


class Give:
    def __init__(self, parts, residual, picks):
        self.residual, self.picks = residual, picks
        capacity = picks.shape[1]
        shapes = [residual.shape] + [(capacity, residual.shape[1])] * (LINE - 1)
        self.own, *away = in_kernel(add_kernel, [parts[0], swap(parts[1])], shapes, "add")
        self.arrived = [hop(part, k + 1) for k, part in enumerate(away)]

    def total(self, *ready):
        total = self.residual.astype(F32) + self.own.astype(F32)
        for pick, part in zip(self.picks, beside(self.arrived, *ready)):
            total += lax.dot_general(pick, part, TN, preferred_element_type=F32)
        return total.astype(BF16)


def silu_parts(pre):
    sig = jax.nn.sigmoid(pre)
    return sig, pre * sig


def backward_factors(pre_gate, pre_up, d_hidden):
    sig, silu = silu_parts(pre_gate)
    d_up = (d_hidden * silu).astype(BF16)
    d_gate = (d_hidden * pre_up * sig * (1.0 + pre_gate * (1.0 - sig))).astype(BF16)
    return d_gate, d_up


def tiles(width):
    tile = TILE if width % TILE == 0 else width
    return [slice(i, i + tile) for i in range(0, width, tile)]


class Stream:
    def __init__(self, groups):
        self.groups = list(groups)
        self.queue = [copy for group in self.groups for copy in group]
        self.start(AHEAD)

    def start(self, count):
        for copy in self.queue[:count]:
            copy.start()
        self.queue = self.queue[count:]

    def take(self):
        group = self.groups.pop(0)
        for copy in group:
            copy.wait()
        self.start(len(group))


def copies(src, dst, sems, axis):
    spans = tiles(src.shape[axis])
    at = (lambda s: (s, slice(None))) if axis == 0 else (lambda s: (slice(None), s))
    return [pltpu.make_async_copy(src.at[at(s)], dst.at[at(s)], sems.at[i]) for i, s in enumerate(spans)]


def rows_in(blocks, x, sems):
    r = blocks[0].shape[0]
    done = [
        pltpu.make_async_copy(b.at[:, : x.shape[1]], x.at[i * r : (i + 1) * r], sems.at[i])
        for i, b in enumerate(blocks)
    ]
    for copy in done:
        copy.start()
    return done


def split_store(value, outs, span):
    r = outs[0].shape[0]
    for i, o in enumerate(outs):
        o[:, span] = value[i * r : (i + 1) * r].astype(BF16)


def forward_kernel(n, *refs):
    blocks, (gate, wg, wu, wd), outs = refs[:n], refs[n : n + 4], refs[n + 4 : 2 * n + 4]
    x, g, u, d, acc_gate, acc_up, s_in, s_g, s_u, s_d = refs[2 * n + 4 :]
    arriving = rows_in(blocks, x, s_in)
    pairs = [list(p) for p in zip(copies(wg, g, s_g, 0), copies(wu, u, s_u, 0))]
    stream = Stream(pairs + [[c] for c in copies(wd, d, s_d, 1)])
    for copy in arriving:
        copy.wait()
    for i, span in enumerate(tiles(g.shape[0])):
        stream.take()
        for w, acc in ((g, acc_gate), (u, acc_up)):
            value = jnp.dot(x[:, span], w[span, :], preferred_element_type=F32)
            acc[...] = value if i == 0 else acc[...] + value
    hidden = (silu_parts(acc_gate[...])[1] * gate[...] * acc_up[...]).astype(BF16)
    for span in tiles(d.shape[1]):
        stream.take()
        split_store(jnp.dot(hidden, d[:, span], preferred_element_type=F32), outs, span)


def pre_kernel(n, *refs):
    blocks, (wg, wu, pre_gate, pre_up) = refs[:n], refs[n : n + 4]
    x, g, u, s_in, s_g, s_u = refs[n + 4 :]
    arriving = rows_in(blocks, x, s_in)
    pairs = [list(p) for p in zip(copies(wg, g, s_g, 0), copies(wu, u, s_u, 0))]
    stream = Stream(pairs)
    for copy in arriving:
        copy.wait()
    for i, span in enumerate(tiles(g.shape[0])):
        stream.take()
        for w, acc in ((g, pre_gate), (u, pre_up)):
            value = jnp.dot(x[:, span], w[span, :], preferred_element_type=F32)
            acc[...] = value if i == 0 else acc[...] + value


def backward_kernel(n, *refs):
    blocks, (gate, pre_gate, pre_up, wg, wu, wd) = refs[:n], refs[n : n + 6]
    outs = refs[n + 6 : 2 * n + 6]
    x, g, u, d, acc, s_in, s_g, s_u, s_d = refs[2 * n + 6 :]
    arriving = rows_in(blocks, x, s_in)
    pairs = [list(p) for p in zip(copies(wg, g, s_g, 0), copies(wu, u, s_u, 0))]
    stream = Stream([[c] for c in copies(wd, d, s_d, 1)] + pairs)
    for copy in arriving:
        copy.wait()
    for i, span in enumerate(tiles(d.shape[1])):
        stream.take()
        value = lax.dot_general(x[:, span], d[:, span], NT, preferred_element_type=F32)
        acc[...] = value if i == 0 else acc[...] + value
    d_gate, d_up = backward_factors(pre_gate[...], pre_up[...], acc[...] * gate[...])
    for span in tiles(g.shape[0]):
        stream.take()
        value = lax.dot_general(d_gate, g[span, :], NT, preferred_element_type=F32)
        value += lax.dot_general(d_up, u[span, :], NT, preferred_element_type=F32)
        split_store(value, outs, span)


def call(kernel, n, args, in_vmem, out_shape, scratch, dots, name):
    anywhere, vmem = pl.BlockSpec(memory_space=pl.ANY), pl.BlockSpec(memory_space=pltpu.VMEM)
    weight = args[-1].size
    return pl.pallas_call(
        lambda *refs: kernel(n, *refs),
        in_specs=[vmem if i in in_vmem else anywhere for i in range(len(args))],
        out_specs=[pl.BlockSpec(memory_space=o.memory_space) for o in out_shape],
        out_shape=out_shape,
        scratch_shapes=scratch,
        compiler_params=pltpu.CompilerParams(vmem_limit_bytes=VMEM_LIMIT),
        cost_estimate=pl.CostEstimate(
            flops=0,
            bytes_accessed=0,
            transcendentals=0,
        ),
        name=name,
    )(*args)


def scratch_of(rows, weights, accs, n):
    width, hid = weights[0].shape
    dma = pltpu.SemaphoreType.DMA
    buffers = [pltpu.VMEM((rows, width), BF16)] + [pltpu.VMEM(w.shape, BF16) for w in weights]
    buffers += [pltpu.VMEM((rows, hid), F32)] * accs
    return buffers + [dma((n,))] + [dma((len(tiles(width)),)) for _ in weights]


def forward_piece(blocks, gate, wg, wu, wd):
    n, r, width = len(blocks), blocks[0].shape[0], wg.shape[0]
    return call(
        forward_kernel,
        n,
        [*blocks, gate, wg, wu, wd],
        (n,),
        [pltpu.VMEM((r, width), BF16)] * n,
        scratch_of(n * r, (wg, wu, wd), 2, n),
        3,
        "forward_piece",
    )


def pre_piece(blocks, wg, wu):
    n, r = len(blocks), blocks[0].shape[0]
    shape = pltpu.VMEM((n * r, wg.shape[1]), F32)
    scratch = scratch_of(n * r, (wg, wu), 0, n)
    return call(pre_kernel, n, [*blocks, wg, wu], (), [shape, shape], scratch, 2, "pre_piece")


def backward_piece(blocks, gate, pre, wg, wu, wd):
    n, r, width = len(blocks), blocks[0].shape[0], wg.shape[0]
    return call(
        backward_kernel,
        n,
        [*blocks, gate, *pre, wg, wu, wd],
        (n, n + 1, n + 2),
        [pltpu.VMEM((r, width), BF16)] * n,
        scratch_of(n * r, (wg, wu, wd), 1, n),
        3,
        "backward_piece",
    )


def level_table(route_ids, gate_levels, token_counts):
    section = lax.axis_index("section")
    sections = lax.axis_size("section")
    experts = lax.axis_size("expert") // SLICES
    routes, levels = route_ids[:, 0], gate_levels[:, 0]
    rows = routes.shape[2]
    first = lambda d, at: lax.dynamic_slice(token_counts[d, :, 0], (at,), (TICKS,))
    counts = jnp.stack([first(0, sections - 1 - section), first(1, section)])
    live = jnp.arange(rows)[None, None, :] < counts[:, :, None]
    named = (routes[..., None] == jnp.arange(experts)) & live[..., None, None]
    table = jnp.sum(jnp.where(named, levels[..., None], 0), axis=3)
    table = jnp.moveaxis(table, 2, 0).reshape(rows, -1).astype(BF16)
    return jnp.pad(table, ((0, 0), (0, -table.shape[1] % LANES)))


def gates_of(tables):
    devices = lax.axis_size("expert")
    experts = devices // SLICES
    mine = lax.axis_index("expert") // SLICES
    levels = tables[:, : 2 * TICKS * experts].astype(F32).reshape(-1, 2 * TICKS, experts)
    sums = jnp.maximum(jnp.sum(levels, axis=2), 1.0)
    own = jnp.sum(jnp.where(jnp.arange(experts) == mine, levels, 0.0), axis=2)
    gates = own / sums
    return [[gates[:, d * TICKS + t][:, None] for t in range(TICKS)] for d in range(2)]


def relay(x, entering, end, turn):
    return jnp.where(lax.axis_index("section") == end, entering, x), turn


def everyone(x):
    return lax.all_gather(x, "expert", axis=0, tiled=True)


def summed(parts, residual):
    parts = lax.psum_scatter(parts, "expert", scatter_dimension=0, tiled=True)
    return (residual.astype(F32) + parts.astype(F32)).astype(BF16)


def whole_line(fwd, bwd, saved, weights, tables, fwd_entering, bwd_entering):
    last = lax.axis_size("section") - 1
    (f_picks0, f_picks1), (b_picks0, b_picks1) = picks_away(tables)
    slots = slot_tables(tables)
    s0, g0 = Gather(saved[0], b_picks0, slots), Gather(bwd, b_picks0)
    f_gates, b_gates = gates_of_slots(tables, slots)
    x0 = Gather(fwd, f_picks0, *s0.arrived)
    pre = pre_piece(s0.blocks(), *weights[:2])
    parts = backward_piece(g0.blocks(), b_gates[0], pre, *weights)
    parts = [*beside(parts[:1], *x0.arrived), parts[1]]
    b0 = Give(parts, bwd, b_picks0)
    parts = forward_piece(x0.blocks(*parts), f_gates[0], *weights)
    f0 = Give(beside(parts, *b0.arrived), fwd, f_picks0)
    s1 = Gather(saved[1], b_picks1, *x0.arrived)
    b_out0 = b0.total()
    bwd1 = turned(*relay(b_out0, bwd_entering[0], 0, -1))
    g1 = Gather(bwd1, b_picks1, *f0.arrived)
    f_out0 = f0.total()
    fwd1 = turned(*relay(f_out0, fwd_entering[0], last, 1))
    pre = pre_piece(s1.blocks(fwd1), *weights[:2])
    x1 = Gather(fwd1, f_picks1, *s1.arrived)
    parts = backward_piece(g1.blocks(), b_gates[1], pre, *weights)
    parts = [*beside(parts[:1], *x1.arrived), parts[1]]
    b1 = Give(parts, bwd1, b_picks1)
    parts = forward_piece(x1.blocks(*parts), f_gates[1], *weights)
    f1 = Give(beside(parts, *b1.arrived), fwd1, f_picks1)
    return [f_out0, f1.total()], [b_out0, b1.total()]


def plain(fwd, bwd, saved, weights, tables, fwd_entering, bwd_entering):
    wg, wu, wd = weights
    last = lax.axis_size("section") - 1

    def dot(a, b):
        return jnp.dot(a, b, preferred_element_type=F32)

    def dot_nt(a, b):
        return lax.dot_general(a, b, NT, preferred_element_type=F32)

    gates = gates_of(everyone(tables))
    fwd_list, bwd_list = [], []
    for tick in range(TICKS):
        x, s, g = everyone(fwd), everyone(saved[tick]), everyone(bwd)
        hidden = silu_parts(dot(x, wg))[1] * gates[0][tick] * dot(x, wu)
        fwd_list.append(summed(dot(hidden.astype(BF16), wd).astype(BF16), fwd))
        d_hidden = dot_nt(g, wd) * gates[1][tick]
        d_gate, d_up = backward_factors(dot(s, wg), dot(s, wu), d_hidden)
        back = dot_nt(d_gate, wg) + dot_nt(d_up, wu)
        bwd_list.append(summed(back.astype(BF16), bwd))
        if tick + 1 < TICKS:
            fwd = turned(*relay(fwd_list[-1], fwd_entering[tick], last, 1))
            bwd = turned(*relay(bwd_list[-1], bwd_entering[tick], 0, -1))
    return fwd_list, bwd_list


def local(
    fwd_arriving,
    fwd_entering,
    bwd_arriving,
    bwd_entering,
    saved_inputs,
    w_gate,
    w_up,
    w_down,
    route_ids,
    gate_levels,
    token_counts,
):
    run = whole_line if on_line() else plain
    fwd_list, bwd_list = run(
        fwd_arriving[0],
        bwd_arriving[0],
        saved_inputs[0],
        (w_gate[0, 0], w_up[0, 0], w_down[0, 0]),
        level_table(route_ids, gate_levels, token_counts),
        fwd_entering,
        bwd_entering,
    )
    return jnp.stack(fwd_list)[None], jnp.stack(bwd_list)[None]


def solution(mesh):
    return jax.shard_map(
        local,
        mesh=mesh,
        in_specs=(
            P("section", "expert", None),
            P(None, "expert", None),
            P("section", "expert", None),
            P(None, "expert", None),
            P("section", None, "expert", None),
            P("section", "expert", None, None),
            P("section", "expert", None, None),
            P("section", "expert", None, None),
            P(None, "section", None, "expert", None),
            P(None, "section", None, "expert", None),
            P(None, None, "expert"),
        ),
        out_specs=(P("section", None, "expert", None), P("section", None, "expert", None)),
        check_vma=False,
    )
```
